32 devices in a mesh: groups: 2 (over y), stores: 4 (over z), weeks: 4 (over x, core).
Axes of the slice: x: 2, y: 2, z: 4, core: 2. Of those that a mesh axis runs over, the one named last changes fastest.
Arguments:
- outcomes: float32 [1024, 8192], P(('groups', 'weeks'), 'stores'), parts along dimension 0, may hold values from -40 to 40
- observed_mask: int32 [1024, 8192], P(('groups', 'weeks'), 'stores'), parts along dimension 0, may hold values 0 or 1
- store_region: int32 [8192], P('stores'), may hold values from 0 to 15
- store_factor: float32 [16384, 128], P(('groups', 'stores')), parts along dimension 0, may hold values from -0.5 to 0.5
- week_factor: float32 [1024, 128], P(('groups', 'weeks')), parts along dimension 0, may hold values from -6 to 6
Outputs:
- imputed: float32 [1024, 8192], P(('groups', 'weeks'), 'stores'), parts along dimension 0
- store_loadings: float32 [16384, 128], P(('groups', 'stores')), parts along dimension 0
- week_loadings: float32 [1024, 128], P(('groups', 'weeks')), parts along dimension 0
The draws below stay inside these ranges and needn't reach their ends.
There are 2 independent parts, one for each index of `groups`. The reference program is written for one: setup_inputs(seed, part) draws one part's arguments, and reference() takes and returns one part's arrays. A program takes and returns all parts, laid end to end along the dimension named above; an argument that names none is the same for every part. Nothing has to cross between parts.
All inputs are finite; a program needn't handle non-finite values. No bound on the sum of `observed_mask` on one device may be relied on, other than what follows from the above.
Results may differ from the reference program's by a relative error of at most 0.00013.
Values sent between devices are 32-bit elements; how exact they have to be, the bound alone decides.
A program may use at most 64 MiB of HBM per device.

```python
import math
import jax
import jax.numpy as jnp
from jax import lax

WEEKS = 512
RANK = 128
REGIONS = 16
ITERS = 2
STORES = 8192


def draw_outcomes(key, part):
    key = jax.random.fold_in(key, 11)
    subkeys = jax.random.split(key, 5)
    position = jnp.arange(STORES, dtype=jnp.float32) / STORES
    store_scale = 0.5 * jnp.exp(math.log(3.0) * position + math.log(4.0) * (jax.random.uniform(subkeys[0], (STORES,)) - 0.5))
    week_scale = jnp.exp(math.log(4.0) * (jax.random.uniform(subkeys[1], (WEEKS,)) - 0.5))
    store_level = jnp.clip(jax.random.normal(subkeys[2], (STORES,)), -3.0, 3.0)
    week_level = jnp.clip(jax.random.normal(subkeys[3], (WEEKS,)), -3.0, 3.0)
    fluctuation = jnp.clip(jax.random.normal(subkeys[4], (WEEKS, STORES)), -5.0, 5.0)
    values = week_scale[:, None] * store_scale[None, :] * fluctuation + store_level[None, :] + week_level[:, None]
    return values.astype(jnp.float32)


def place_ends(result, rng, low, largest):
    dims = result.shape
    place = [jax.random.randint(jax.random.fold_in(rng, axis), (), 0, dims[axis]) for axis in range(len(dims))]
    result = result.at[tuple(place)].set(low)
    longest = dims.index(max(dims))
    place[longest] = (place[longest] + 1) % dims[longest]
    return result.at[tuple(place)].set(largest)


def level_of(rng, extent, cuts, low, high):
    level = 1.0
    for axis_at, blocks in cuts:
        draws = jax.random.uniform(jax.random.fold_in(jax.random.fold_in(rng, 6), axis_at), (blocks,), jnp.float32, low / len(cuts), high / len(cuts))
        level = level * jnp.repeat(jnp.exp(draws), extent[axis_at] // blocks).reshape((-1,) + (1,) * (len(extent) - 1 - axis_at))
    return level


def normal_values(own_key, extent, scale, most, shards=(), kind=jnp.bfloat16):
    entries = jax.random.normal(own_key, extent, jnp.float32) * scale
    if len(shards) > 0:
        entries = level_of(own_key, extent, shards, -0.22, 0.18) * entries
    return jnp.clip(entries, min=-most, max=most).astype(kind)


def setup_inputs(seed: int = 0, part: int = 0) -> dict:
    key_list = jax.random.split(jax.random.key(seed), 6)
    own_keys = jax.random.split(jax.random.fold_in(key_list[5], part), 6)
    return {
        "outcomes": draw_outcomes(jax.random.fold_in(jax.random.fold_in(key_list[5], part), 71), part),
        "observed_mask": place_ends((jax.random.randint(own_keys[1], (WEEKS, STORES), 0, 10) < 7).astype(jnp.int32), jax.random.fold_in(own_keys[1], 1), 0, 1),
        "store_region": place_ends(jax.random.randint(key_list[2], (STORES,), 0, REGIONS), jax.random.fold_in(key_list[2], 1), 0, REGIONS - 1).astype(jnp.int32),
        "store_factor": normal_values(own_keys[3], (STORES, RANK), RANK ** -0.5, 0.5, ((0, 4),), jnp.float32),
        "week_factor": normal_values(own_keys[4], (WEEKS, RANK), 1.0, 6.0, ((0, 4),), jnp.float32),
    }


PRECISE = lax.Precision.HIGHEST
RIDGE_WEIGHT = 8.0

def gram_inverse(gram):
    identity = jnp.eye(gram.shape[0], dtype=gram.dtype)
    lower_factor = jnp.linalg.cholesky(gram + RIDGE_WEIGHT * identity)
    lower_inverse = lax.linalg.triangular_solve(lower_factor, identity, left_side=True, lower=True)
    return jnp.dot(lower_inverse.T, lower_inverse, precision=PRECISE)

def reference(outcomes, observed_mask, store_region, store_factor, week_factor):
    observed = observed_mask.astype(jnp.float32)
    onehot = (store_region[:, None] == jnp.arange(REGIONS, dtype=jnp.int32)[None, :]).astype(outcomes.dtype)
    week_count = jnp.dot(observed.astype(outcomes.dtype), onehot, precision=PRECISE)
    region_effect = jnp.dot(observed * outcomes, onehot, precision=PRECISE) / (week_count + 1.0)
    region_cells = jnp.dot(region_effect, onehot.T, precision=PRECISE)
    store_count = jnp.sum(observed, axis=0)
    store_effect = jnp.sum(observed * (outcomes - region_cells), axis=0) / (store_count + 1.0)
    centered = outcomes - region_cells - store_effect[None, :]
    factor_store = store_factor
    factor_week = week_factor
    for iteration in range(ITERS):
        residual = observed * (centered - jnp.dot(factor_week, factor_store.T, precision=PRECISE))
        store_gram = jnp.dot(factor_store.T, factor_store, precision=PRECISE)
        product = jnp.dot(residual, factor_store, precision=PRECISE)
        factor_week = jnp.dot(product + jnp.dot(factor_week, store_gram, precision=PRECISE), gram_inverse(store_gram), precision=PRECISE)
        residual = observed * (centered - jnp.dot(factor_week, factor_store.T, precision=PRECISE))
        week_gram = jnp.dot(factor_week.T, factor_week, precision=PRECISE)
        product = jnp.dot(residual.T, factor_week, precision=PRECISE)
        factor_store = jnp.dot(product + jnp.dot(factor_store, week_gram, precision=PRECISE), gram_inverse(week_gram), precision=PRECISE)
    imputed = region_cells + store_effect[None, :] + jnp.dot(factor_week, factor_store.T, precision=PRECISE)
    return (imputed, factor_store, factor_week)
```

```python
import functools

import jax
import jax.numpy as jnp
from jax import lax
from jax.experimental import pallas as pl
from jax.experimental.pallas import tpu as pltpu
from jax.sharding import PartitionSpec as P

REGIONS = 16
ITERS = 2
RIDGE_WEIGHT = 8.0
PANEL = 16
MESH = pl.DeviceIdType.MESH
PRECISE = lax.Precision.HIGHEST


def dot(a, b, ca=1, cb=0):
    return lax.dot_general(
        a, b, (((ca,), (cb,)), ((), ())), precision=PRECISE, preferred_element_type=jnp.float32
    )


def inverse(gram, work):
    rank = gram.shape[0]
    row_at = lax.broadcasted_iota(jnp.int32, (rank, rank), 0)
    lane_at = lax.broadcasted_iota(jnp.int32, (rank, rank), 1)
    work[...] = gram + jnp.where(row_at == lane_at, RIDGE_WEIGHT, 0.0)
    panel_row = lax.broadcasted_iota(jnp.int32, (PANEL, rank), 0)
    panel_lane = lax.broadcasted_iota(jnp.int32, (PANEL, rank), 1)

    def step(_, carry):
        matrix = work[...]
        panel = matrix[:PANEL, :]
        for j in range(PANEL):
            pivot = 1.0 / panel[j : j + 1, j : j + 1]
            row = jnp.where(panel_lane[:1] == j, pivot, panel[j : j + 1, :] * pivot)
            column = panel[:, j : j + 1]
            cleared = jnp.where(panel_lane == j, 0.0, panel)
            panel = jnp.where(panel_row == j, row, cleared - column * row)
        rest = matrix[PANEL:, :]
        kept = jnp.where(lane_at[PANEL:] < PANEL, 0.0, rest)
        rest = kept - dot(rest[:, :PANEL], panel)
        work[...] = pltpu.roll(jnp.concatenate([rest, panel], axis=0), rank - PANEL, 1)
        return carry

    lax.fori_loop(0, rank // PANEL, step, 0)
    return work[...]


class Sum:
    def __init__(self, axis, n, me, refs):
        self.axis, self.n, self.me = axis, n, me
        self.send, self.part, self.full, self.sems = refs
        self.rows = self.send.shape[0] // n
        self.direct = self.rows < 8

    @staticmethod
    def scratch(n, rank):
        rows = rank // n
        part = (n, rank, rank) if rows < 8 else (n, rows, rank)
        return [
            pltpu.VMEM((rank, rank), jnp.float32),
            pltpu.VMEM(part, jnp.float32),
            pltpu.VMEM((rank, rank), jnp.float32),
            pltpu.SemaphoreType.DMA((4, n)),
        ]

    def block(self, ref, owner):
        return ref.at[pl.ds(pl.multiple_of(owner * self.rows, 8), self.rows)]

    def first(self, j):
        peer = lax.rem(self.me + j, self.n)
        source = self.send if self.direct else self.block(self.send, peer)
        return pltpu.make_async_remote_copy(
            source, self.part.at[j], self.sems.at[0, j], self.sems.at[1, j],
            device_id={self.axis: peer}, device_id_type=MESH,
        )

    def second(self, j, arriving):
        owner = lax.rem(self.me + self.n - j, self.n) if arriving else self.me
        peer = lax.rem(self.me + j, self.n)
        block = self.block(self.full, owner)
        return pltpu.make_async_remote_copy(
            block, block, self.sems.at[2, j], self.sems.at[3, j],
            device_id={self.axis: peer}, device_id_type=MESH,
        )

    def start(self, value):
        self.send[...] = value
        for j in range(1, self.n):
            self.first(j).start()

    def spread(self):
        if self.direct:
            return
        total = self.block(self.send, self.me)[...]
        for j in range(1, self.n):
            self.first(j).wait_recv()
            total = total + self.part[j]
        self.block(self.full, self.me)[...] = total
        for j in range(1, self.n):
            self.second(j, False).start()

    def result(self):
        if not self.direct:
            for j in range(1, self.n):
                self.second(j, True).wait_recv()
            return self.full[...]
        for j in range(1, self.n):
            self.first(j).wait_recv()
        self.part[0] = self.send[...]

        def body(t, total):
            return total + self.part[lax.rem(self.n - t + self.me, self.n)]

        return lax.fori_loop(0, self.n, body, jnp.zeros(self.send.shape, jnp.float32))

    def drain(self):
        for j in range(1, self.n):
            self.first(j).wait_send()
            if not self.direct:
                self.second(j, False).wait_send()


def fused(nz, nw, n_sum, *refs):
    (outcomes, mask, region, a_first, b_first, imputed, a_out, b_out) = refs[:8]
    refs = refs[8:]
    (onehot, obs, cent, base, pred, obs_t, cent_t, work, region_buf, store_buf, effect_row,
     region_sems, store_sems) = refs[:13]
    refs = refs[13:]
    (sib_send, sib_recv, x_send, x_recv, own, a_all, sib_sems, x_sems, ax_sems, as_sems) = refs[:10]
    refs = refs[10:]
    z = lax.axis_index("stores")
    w = lax.axis_index("weeks")
    sums = []
    for k in range(4 * ITERS - ITERS):
        over_z = k % 3 < 2
        group = refs[4 * k : 4 * k + 4]
        sums.append(Sum("stores", nz, z, group) if over_z else Sum("weeks", nw, w, group))
    weeks, stores = outcomes.shape
    rank = b_first.shape[1]
    core, chip, chips = lax.rem(w, 2), w // 2, nw // 2
    half = stores // 2
    sub = half // chips
    tile = 128
    per_sub = sub // tile
    n_tiles = half // tile
    n_away = n_tiles - per_sub
    wide = stores // 4

    barrier = pltpu.get_barrier_semaphore()
    for j in range(1, nz):
        pl.semaphore_signal(barrier, device_id={"stores": lax.rem(z + j, nz)}, device_id_type=MESH)
    for j in range(1, nw):
        pl.semaphore_signal(barrier, device_id={"weeks": lax.rem(w + j, nw)}, device_id_type=MESH)

    onehot[...] = (
        lax.broadcasted_iota(jnp.int32, (REGIONS, stores), 0) == region[...]
    ).astype(jnp.float32)
    obs[...] = mask[...].astype(jnp.float32)
    total = dot(onehot[...], obs[...] * outcomes[...], 1, 1)
    count = dot(onehot[...], obs[...], 1, 1)
    region_buf[0] = jnp.concatenate([total, count], axis=0)
    pl.semaphore_wait(barrier, nz + nw - 2)

    def region_copy(j):
        return pltpu.make_async_remote_copy(
            region_buf.at[0], region_buf.at[j], region_sems.at[0, j], region_sems.at[1, j],
            device_id={"stores": lax.rem(z + j, nz)}, device_id_type=MESH,
        )

    for j in range(1, nz):
        region_copy(j).start()

    def gram_of(ref):
        def body(t, total):
            block = ref[pl.ds(pl.multiple_of(t * 256, 256), 256), :]
            return total + dot(block.T, block)

        return lax.fori_loop(0, stores // 256, body, jnp.zeros((rank, rank), jnp.float32))

    sums[0].start(gram_of(a_first))

    for j in range(1, nz):
        region_copy(j).wait_recv()

    def add_region(t, total):
        return total + region_buf[lax.rem(z - t + nz, nz)]

    sums_region = lax.fori_loop(
        0, nz, add_region, jnp.zeros(region_buf.shape[1:], jnp.float32)
    )
    effect = (sums_region[:REGIONS] / (sums_region[REGIONS:] + 1.0)).T
    base[...] = dot(effect, onehot[...])
    store_total = jnp.sum(obs[...] * (outcomes[...] - base[...]), axis=0, keepdims=True)
    store_count = jnp.sum(obs[...], axis=0, keepdims=True)
    for q in range(4):
        store_buf[0, q : q + 1, :] = store_total[:, q * wide : (q + 1) * wide]
        store_buf[0, q + 4 : q + 5, :] = store_count[:, q * wide : (q + 1) * wide]

    def store_copy(j):
        return pltpu.make_async_remote_copy(
            store_buf.at[0], store_buf.at[j], store_sems.at[0, j], store_sems.at[1, j],
            device_id={"weeks": lax.rem(w + j, nw)}, device_id_type=MESH,
        )

    for j in range(1, nw):
        store_copy(j).start()
    sums[0].spread()

    def predict(b_value, ref):
        def body(t, carry):
            at = pl.ds(pl.multiple_of(t * 256, 256), 256)
            pred[:, at] = dot(b_value, ref[at, :], 1, 1)
            return carry

        lax.fori_loop(0, stores // 256, body, 0)

    predict(b_first[...], a_first)

    def turn(source, target):
        def body(t, carry):
            at = pl.ds(pl.multiple_of(t * 128, 128), 128)
            target[at, :] = source[:, at].T
            return carry

        lax.fori_loop(0, stores // 128, body, 0)

    turn(obs, obs_t)
    for j in range(1, nw):
        store_copy(j).wait_recv()

    def add_store(t, total):
        return total + store_buf[lax.rem(w - t + nw, nw)]

    sums_store = lax.fori_loop(0, nw, add_store, jnp.zeros(store_buf.shape[1:], jnp.float32))
    effect_s = sums_store[:4] / (sums_store[4:] + 1.0)
    for q in range(4):
        effect_row[:, q * wide : (q + 1) * wide] = effect_s[q : q + 1]
    base[...] = base[...] + effect_row[...]
    cent[...] = obs[...] * (outcomes[...] - base[...])

    b_value = b_first[...]
    a_ref = a_first
    for it in range(ITERS):
        sum_gram, sum_product, sum_week = sums[3 * it : 3 * it + 3]
        if it > 0:
            sum_gram.start(gram_of(a_ref))
            predict(b_value, a_ref)

        def product_step(t, total):
            at = pl.ds(pl.multiple_of(t * 256, 256), 256)
            residual = cent[:, at] - obs[:, at] * pred[:, at]
            return total + dot(residual, a_ref[at, :])

        product = lax.fori_loop(
            0, stores // 256, product_step, jnp.zeros((weeks, rank), jnp.float32)
        )
        if weeks < rank:
            product = jnp.concatenate(
                [product, jnp.zeros((rank - weeks, rank), jnp.float32)], axis=0
            )
        sum_product.start(product)
        if it > 0:
            sum_gram.spread()
        gram = sum_gram.result()
        if it == 0:
            turn(cent, cent_t)
        sum_product.spread()
        inv = inverse(gram, work)
        product = sum_product.result()[:weeks]
        b_value = dot(product + dot(b_value, gram), inv)

        sum_week.start(dot(b_value.T, b_value))

        def rows_of(i):
            to = lax.rem(chip + 1 + i // per_sub, chips)
            return pl.multiple_of(to * sub + lax.rem(i, per_sub) * tile, tile)

        def local_product(row):
            at = pl.ds(pl.multiple_of(row, tile), tile)
            predicted = dot(a_ref[at, :], b_value, 1, 1)
            return dot(cent_t[at, :] - obs_t[at, :] * predicted, b_value)

        def sib_copy(i):
            at = pl.ds(rows_of(i), tile)
            return pltpu.make_async_remote_copy(
                sib_send.at[it, at], sib_recv.at[it, at],
                sib_sems.at[it, 0, i], sib_sems.at[it, 1, i],
                device_id={"weeks": chip * 2 + 1 - core}, device_id_type=MESH,
            )

        def x_copy(i):
            to = lax.rem(chip + 1 + i // per_sub, chips)
            return pltpu.make_async_remote_copy(
                x_send.at[it, pl.ds(pl.multiple_of(i * tile, tile), tile)],
                x_recv.at[it, pl.ds(pl.multiple_of(i * tile, tile), tile)],
                x_sems.at[it, 0, i], x_sems.at[it, 1, i],
                device_id={"weeks": to * 2 + core}, device_id_type=MESH,
            )

        def to_sibling(i, carry):
            sib_send[it, pl.ds(rows_of(i), tile)] = local_product((1 - core) * half + rows_of(i))
            sib_copy(i).start()
            return carry

        def chip_sum(i):
            mine = local_product(core * half + rows_of(i))
            sib_copy(i).wait_recv()
            theirs = sib_recv[it, pl.ds(rows_of(i), tile)]
            return mine + theirs

        def to_chips(i, carry):
            x_send[it, pl.ds(pl.multiple_of(i * tile, tile), tile)] = chip_sum(i)
            x_copy(i).start()
            return carry

        def keep(i, carry):
            own[pl.ds(pl.multiple_of((i - n_away) * tile, tile), tile)] = chip_sum(i)
            return carry

        lax.fori_loop(0, n_away, to_sibling, 0)
        lax.fori_loop(0, n_away, to_chips, 0)
        sum_week.spread()
        lax.fori_loop(n_away, n_tiles, to_sibling, 0)
        lax.fori_loop(n_away, n_tiles, keep, 0)
        week_gram = sum_week.result()
        inv = inverse(week_gram, work)

        def a_copy_x(d, q, arriving):
            owner = lax.rem(chip + chips - d, chips) if arriving else chip
            at = pl.ds(pl.multiple_of(core * half + owner * sub + q * tile, tile), tile)
            return pltpu.make_async_remote_copy(
                a_all.at[it, at], a_all.at[it, at],
                ax_sems.at[it, 0, d, q], ax_sems.at[it, 1, d, q],
                device_id={"weeks": lax.rem(chip + d, chips) * 2 + core}, device_id_type=MESH,
            )

        def a_copy_sib(d, q, arriving):
            owner = lax.rem(chip + chips - d, chips)
            part = 1 - core if arriving else core
            at = pl.ds(pl.multiple_of(part * half + owner * sub + q * tile, tile), tile)
            return pltpu.make_async_remote_copy(
                a_all.at[it, at], a_all.at[it, at],
                as_sems.at[it, 0, d, q], as_sems.at[it, 1, d, q],
                device_id={"weeks": chip * 2 + 1 - core}, device_id_type=MESH,
            )

        def update(q, carry):
            at = pl.ds(pl.multiple_of(q * tile, tile), tile)
            total = own[at]
            for d in range(1, chips):
                i = (d - 1) * per_sub + q
                x_copy(i).wait_recv()
                total = total + x_recv[it, pl.ds(pl.multiple_of(i * tile, tile), tile)]
            rows = pl.ds(pl.multiple_of(core * half + chip * sub + q * tile, tile), tile)
            a_all[it, rows] = dot(total + dot(a_ref[rows, :], week_gram), inv)
            for d in range(1, chips):
                a_copy_x(d, q, False).start()
            a_copy_sib(0, q, False).start()
            return carry

        def forward(q, carry):
            for d in range(1, chips):
                a_copy_x(d, q, True).wait_recv()
                a_copy_sib(d, q, False).start()
            return carry

        def arrive(q, carry):
            for d in range(chips):
                a_copy_sib(d, q, True).wait_recv()
            return carry

        lax.fori_loop(0, per_sub, update, 0)
        lax.fori_loop(0, per_sub, forward, 0)
        lax.fori_loop(0, per_sub, arrive, 0)

        def drain_tiles(i, carry):
            sib_copy(i).wait_send()
            return carry

        def drain_away(i, carry):
            x_copy(i).wait_send()
            return carry

        def drain_rows(q, carry):
            for d in range(chips):
                if d > 0:
                    a_copy_x(d, q, False).wait_send()
                a_copy_sib(d, q, False).wait_send()
            return carry

        lax.fori_loop(0, n_tiles, drain_tiles, 0)
        lax.fori_loop(0, n_away, drain_away, 0)
        lax.fori_loop(0, per_sub, drain_rows, 0)
        a_ref = a_all.at[it]

    b_out[...] = b_value

    def finish(t, carry):
        at = pl.ds(pl.multiple_of(t * 256, 256), 256)
        block = a_ref[at, :]
        a_out[at, :] = block
        imputed[:, at] = base[:, at] + dot(b_value, block, 1, 1)
        return carry

    lax.fori_loop(0, stores // 256, finish, 0)
    for j in range(1, nz):
        region_copy(j).wait_send()
    for j in range(1, nw):
        store_copy(j).wait_send()
    for item in sums:
        item.drain()


def on_device(nz, nw, outcomes, observed_mask, store_region, store_factor, week_factor):
    weeks, stores = outcomes.shape
    rank = week_factor.shape[1]
    chips = nw // 2
    half = stores // 2
    n_tiles = half // 128
    per_sub = n_tiles // chips
    away = max(half - half // chips, 128)
    vmem = lambda *shape: pltpu.VMEM(shape, jnp.float32)
    sems = lambda *shape: pltpu.SemaphoreType.DMA(shape)
    scratch = [
        vmem(REGIONS, stores),
        vmem(weeks, stores), vmem(weeks, stores), vmem(weeks, stores), vmem(weeks, stores),
        vmem(stores, weeks), vmem(stores, weeks),
        vmem(rank, rank),
        vmem(nz, 2 * REGIONS, weeks), vmem(nw, 8, stores // 4), vmem(1, stores),
        sems(2, nz), sems(2, nw),
        vmem(ITERS, half, rank), vmem(ITERS, half, rank),
        vmem(ITERS, away, rank), vmem(ITERS, away, rank),
        vmem(half // chips, rank),
        vmem(ITERS, stores, rank),
        sems(ITERS, 2, n_tiles), sems(ITERS, 2, n_tiles),
        sems(ITERS, 2, chips, per_sub), sems(ITERS, 2, chips, per_sub),
    ]
    for _ in range(ITERS):
        scratch += Sum.scratch(nz, rank) + Sum.scratch(nz, rank) + Sum.scratch(nw, rank)
    shape = lambda *dims: jax.ShapeDtypeStruct(dims, jnp.float32)
    return pl.pallas_call(
        functools.partial(fused, nz, nw, 3 * ITERS),
        out_shape=(shape(weeks, stores), shape(stores, rank), shape(weeks, rank)),
        in_specs=[pl.BlockSpec(memory_space=pltpu.VMEM)] * 5,
        out_specs=tuple([pl.BlockSpec(memory_space=pltpu.VMEM)] * 3),
        scratch_shapes=scratch,
        compiler_params=pltpu.CompilerParams(
            collective_id=0, has_side_effects=True, vmem_limit_bytes=48 * 1024 * 1024
        ),
    )(outcomes, observed_mask, store_region.reshape(1, stores), store_factor, week_factor)


def solution(mesh):
    placed = (
        P(("groups", "weeks"), "stores"),
        P(("groups", "weeks"), "stores"),
        P("stores"),
        P(("groups", "stores"), None),
        P(("groups", "weeks"), None),
    )
    return jax.shard_map(
        functools.partial(on_device, mesh.shape["stores"], mesh.shape["weeks"]),
        mesh=mesh,
        in_specs=placed,
        out_specs=(
            P(("groups", "weeks"), "stores"),
            P(("groups", "stores"), None),
            P(("groups", "weeks"), None),
        ),
        check_vma=False,
    )
```

```python
import functools

import jax
import jax.numpy as jnp
from jax import lax
from jax.experimental import pallas as pl
from jax.experimental.pallas import tpu as pltpu
from jax.sharding import PartitionSpec as P

REGIONS = 16
ITERS = 2
RIDGE_WEIGHT = 8.0
PANEL = 16
MESH = pl.DeviceIdType.MESH
PRECISE = lax.Precision.HIGHEST


def dot(a, b, ca=1, cb=0):
    return lax.dot_general(
        a, b, (((ca,), (cb,)), ((), ())), precision=PRECISE, preferred_element_type=jnp.float32
    )


def split(x):
    high = x.astype(jnp.bfloat16)
    return high, (x - high.astype(jnp.float32)).astype(jnp.bfloat16)


def dot1(a, b, ca=1, cb=0):
    return lax.dot_general(a, b, (((ca,), (cb,)), ((), ())), preferred_element_type=jnp.float32)


def dot3(a, b, ca=1, cb=0):
    a_high, a_low = split(a)
    b_high, b_low = split(b)
    return (
        dot1(a_high, b_high, ca, cb) + dot1(a_high, b_low, ca, cb) + dot1(a_low, b_high, ca, cb)
    )


def inverse(gram, work):
    rank = gram.shape[0]
    row_at = lax.broadcasted_iota(jnp.int32, (rank, rank), 0)
    lane_at = lax.broadcasted_iota(jnp.int32, (rank, rank), 1)
    work[...] = gram + jnp.where(row_at == lane_at, RIDGE_WEIGHT, 0.0)
    panel_row = lax.broadcasted_iota(jnp.int32, (PANEL, rank), 0)
    panel_lane = lax.broadcasted_iota(jnp.int32, (PANEL, rank), 1)

    def step(_, carry):
        matrix = work[...]
        panel = matrix[:PANEL, :]
        columns = [jnp.broadcast_to(panel[:, j : j + 1], panel.shape) for j in range(PANEL)]
        for k in range(PANEL):
            pivot = 1.0 / columns[k][k : k + 1, :]
            column = columns[k]
            row = jnp.where(panel_lane[:1] == k, pivot, panel[k : k + 1, :] * pivot)
            cleared = jnp.where(panel_lane == k, 0.0, panel)
            panel = jnp.where(panel_row == k, row, cleared - column * row)
            for j in range(k + 1, PANEL):
                scaled = columns[j][k : k + 1, :] * pivot
                columns[j] = jnp.where(panel_row == k, scaled, columns[j] - column * scaled)
        rest = matrix[PANEL:, :]
        kept = jnp.where(lane_at[PANEL:] < PANEL, 0.0, rest)
        rest = kept - dot(rest[:, :PANEL], panel)
        work[...] = pltpu.roll(jnp.concatenate([rest, panel], axis=0), rank - PANEL, 1)
        return carry

    lax.fori_loop(0, rank // PANEL, step, 0)
    return work[...]


class Sum:
    def __init__(self, axis, n, me, refs):
        self.axis, self.n, self.me = axis, n, me
        self.send, self.part, self.full, self.sems = refs
        self.rows = self.send.shape[0] // n
        self.direct = self.rows < 8

    @staticmethod
    def scratch(n, rank):
        rows = rank // n
        part = (n, rank, rank) if rows < 8 else (n, rows, rank)
        return [
            pltpu.VMEM((rank, rank), jnp.float32),
            pltpu.VMEM(part, jnp.float32),
            pltpu.VMEM((rank, rank), jnp.float32),
            pltpu.SemaphoreType.DMA((4, n)),
        ]

    def block(self, ref, owner):
        return ref.at[pl.ds(pl.multiple_of(owner * self.rows, 8), self.rows)]

    def first(self, j):
        peer = lax.rem(self.me + j, self.n)
        source = self.send if self.direct else self.block(self.send, peer)
        return pltpu.make_async_remote_copy(
            source, self.part.at[j], self.sems.at[0, j], self.sems.at[1, j],
            device_id={self.axis: peer}, device_id_type=MESH,
        )

    def second(self, j, arriving):
        owner = lax.rem(self.me + self.n - j, self.n) if arriving else self.me
        peer = lax.rem(self.me + j, self.n)
        block = self.block(self.full, owner)
        return pltpu.make_async_remote_copy(
            block, block, self.sems.at[2, j], self.sems.at[3, j],
            device_id={self.axis: peer}, device_id_type=MESH,
        )

    def start(self, value):
        self.send[...] = value
        for j in range(1, self.n):
            self.first(j).start()

    def spread(self):
        if self.direct:
            return
        total = self.block(self.send, self.me)[...]
        for j in range(1, self.n):
            self.first(j).wait_recv()
            total = total + self.part[j]
        self.block(self.full, self.me)[...] = total
        for j in range(1, self.n):
            self.second(j, False).start()

    def result(self):
        if not self.direct:
            for j in range(1, self.n):
                self.second(j, True).wait_recv()
            return self.full[...]
        for j in range(1, self.n):
            self.first(j).wait_recv()
        self.part[0] = self.send[...]

        def body(t, total):
            return total + self.part[lax.rem(self.n - t + self.me, self.n)]

        return lax.fori_loop(0, self.n, body, jnp.zeros(self.send.shape, jnp.float32))

    def drain(self):
        for j in range(1, self.n):
            self.first(j).wait_send()
            if not self.direct:
                self.second(j, False).wait_send()


def fused(nz, nw, n_sum, *refs):
    hbm_in, hbm_out = refs[:5], refs[5:8]
    (outcomes, mask, region, a_first, b_first, imputed, b_last, in_sems, out_sems) = refs[8:17]
    refs = refs[17:]
    loads = [
        pltpu.make_async_copy(source, target, in_sems.at[k])
        for k, (source, target) in enumerate(
            zip(hbm_in, (outcomes, mask, region, a_first, b_first))
        )
    ]
    for k in (2, 1, 0, 3, 4):
        loads[k].start()
    (onehot, obs, cent, base, pred, obs_t, cent_t, work, region_buf, store_buf, effect_row,
     region_sems, store_sems) = refs[:13]
    refs = refs[13:]
    (sib_send, sib_recv, x_send, x_recv, own, a_all, sib_sems, x_sems, ax_sems, as_sems) = refs[:10]
    refs = refs[10:]
    z = lax.axis_index("stores")
    w = lax.axis_index("weeks")
    sums = []
    for k in range(4 * ITERS - ITERS):
        over_z = k % 3 < 2
        group = refs[4 * k : 4 * k + 4]
        sums.append(Sum("stores", nz, z, group) if over_z else Sum("weeks", nw, w, group))
    weeks, stores = outcomes.shape
    rank = b_first.shape[1]
    core, chip, chips = lax.rem(w, 2), w // 2, nw // 2
    half = stores // 2
    sub = half // chips
    tile = min(256, sub)
    per_sub = sub // tile
    n_tiles = half // tile
    n_away = n_tiles - per_sub
    wide = stores // 4
    big = stores // 2
    step = stores // 4

    b_store = pltpu.make_async_copy(b_last, hbm_out[2], out_sems.at[0])
    barrier = pltpu.get_barrier_semaphore()
    for j in range(1, nz):
        pl.semaphore_signal(barrier, device_id={"stores": lax.rem(z + j, nz)}, device_id_type=MESH)
    for j in range(1, nw):
        pl.semaphore_signal(barrier, device_id={"weeks": lax.rem(w + j, nw)}, device_id_type=MESH)

    for k in (2, 1, 0):
        loads[k].wait()
    onehot[...] = (
        lax.broadcasted_iota(jnp.int32, (REGIONS, stores), 0) == region[...]
    ).astype(jnp.bfloat16)
    obs[...] = mask[...].astype(jnp.float32)
    high, low = split(obs[...] * outcomes[...])
    total = dot1(onehot[...], high, 1, 1) + dot1(onehot[...], low, 1, 1)
    count = dot1(onehot[...], obs[...].astype(jnp.bfloat16), 1, 1)
    region_buf[0] = jnp.concatenate([total, count], axis=0)
    pl.semaphore_wait(barrier, nz + nw - 2)

    def region_copy(j):
        return pltpu.make_async_remote_copy(
            region_buf.at[0], region_buf.at[j], region_sems.at[0, j], region_sems.at[1, j],
            device_id={"stores": lax.rem(z + j, nz)}, device_id_type=MESH,
        )

    for j in range(1, nz):
        region_copy(j).start()

    def gram_step(t, total):
        block = a_first[pl.ds(pl.multiple_of(t * big, big), big), :]
        return total + dot3(block, block, 0, 0)

    loads[3].wait()
    loads[4].wait()
    zero = jnp.zeros((rank, rank), jnp.float32)
    sums[0].start(lax.fori_loop(0, stores // big, gram_step, zero))

    for j in range(1, nz):
        region_copy(j).wait_recv()

    def add_region(t, total):
        return total + region_buf[lax.rem(z - t + nz, nz)]

    sums_region = lax.fori_loop(
        0, nz, add_region, jnp.zeros(region_buf.shape[1:], jnp.float32)
    )
    effect = (sums_region[:REGIONS] / (sums_region[REGIONS:] + 1.0)).T
    high, low = split(effect)
    base[...] = dot1(high, onehot[...]) + dot1(low, onehot[...])
    store_total = jnp.sum(obs[...] * (outcomes[...] - base[...]), axis=0, keepdims=True)
    store_count = jnp.sum(obs[...], axis=0, keepdims=True)
    for q in range(4):
        store_buf[0, q : q + 1, :] = store_total[:, q * wide : (q + 1) * wide]
        store_buf[0, q + 4 : q + 5, :] = store_count[:, q * wide : (q + 1) * wide]

    def store_copy(j):
        return pltpu.make_async_remote_copy(
            store_buf.at[0], store_buf.at[j], store_sems.at[0, j], store_sems.at[1, j],
            device_id={"weeks": lax.rem(w + j, nw)}, device_id_type=MESH,
        )

    for j in range(1, nw):
        store_copy(j).start()
    sums[0].spread()

    b_value = b_first[...]

    def predict_step(t, carry):
        at = pl.ds(pl.multiple_of(t * step, step), step)
        pred[:, at] = dot3(b_value, a_first[at, :], 1, 1)
        return carry

    lax.fori_loop(0, stores // step, predict_step, 0)

    def turn(source, target):
        def body(t, carry):
            at = pl.ds(pl.multiple_of(t * step, step), step)
            target[at, :] = source[:, at].T
            return carry

        lax.fori_loop(0, stores // step, body, 0)

    turn(obs, obs_t)
    for j in range(1, nw):
        store_copy(j).wait_recv()

    def add_store(t, total):
        return total + store_buf[lax.rem(w - t + nw, nw)]

    sums_store = lax.fori_loop(0, nw, add_store, jnp.zeros(store_buf.shape[1:], jnp.float32))
    effect_s = sums_store[:4] / (sums_store[4:] + 1.0)
    for q in range(4):
        effect_row[:, q * wide : (q + 1) * wide] = effect_s[q : q + 1]
    base[...] = base[...] + effect_row[...]
    cent[...] = obs[...] * (outcomes[...] - base[...])

    def product_step(t, total):
        at = pl.ds(pl.multiple_of(t * big, big), big)
        residual = cent[:, at] - obs[:, at] * pred[:, at]
        return total + dot3(residual, a_first[at, :])

    product = lax.fori_loop(
        0, stores // big, product_step, jnp.zeros((weeks, rank), jnp.float32)
    )
    gram = None
    a_ref = a_first
    for it in range(ITERS):
        sum_gram, sum_product, sum_week = sums[3 * it : 3 * it + 3]
        if it > 0:
            sum_gram.start(gram)
        if weeks < rank:
            product = jnp.concatenate(
                [product, jnp.zeros((rank - weeks, rank), jnp.float32)], axis=0
            )
        sum_product.start(product)
        if it > 0:
            sum_gram.spread()
        gram = sum_gram.result()
        if it == 0:
            turn(cent, cent_t)
        sum_product.spread()
        inv = inverse(gram, work)
        product = sum_product.result()[:weeks]
        b_value = dot(product + dot(b_value, gram), inv)

        sum_week.start(dot(b_value.T, b_value))

        def rows_of(i):
            to = lax.rem(chip + 1 + i // per_sub, chips)
            return pl.multiple_of(to * sub + lax.rem(i, per_sub) * tile, tile)

        def local_product(row):
            at = pl.ds(pl.multiple_of(row, tile), tile)
            predicted = dot3(a_ref[at, :], b_value, 1, 1)
            return dot3(cent_t[at, :] - obs_t[at, :] * predicted, b_value)

        def sib_copy(i):
            at = pl.ds(rows_of(i), tile)
            return pltpu.make_async_remote_copy(
                sib_send.at[it, at], sib_recv.at[it, at],
                sib_sems.at[it, 0, i], sib_sems.at[it, 1, i],
                device_id={"weeks": chip * 2 + 1 - core}, device_id_type=MESH,
            )

        def x_copy(i):
            to = lax.rem(chip + 1 + i // per_sub, chips)
            return pltpu.make_async_remote_copy(
                x_send.at[it, pl.ds(pl.multiple_of(i * tile, tile), tile)],
                x_recv.at[it, pl.ds(pl.multiple_of(i * tile, tile), tile)],
                x_sems.at[it, 0, i], x_sems.at[it, 1, i],
                device_id={"weeks": to * 2 + core}, device_id_type=MESH,
            )

        def to_sibling(i, carry):
            sib_send[it, pl.ds(rows_of(i), tile)] = local_product((1 - core) * half + rows_of(i))
            sib_copy(i).start()
            return carry

        def chip_sum(i):
            mine = local_product(core * half + rows_of(i))
            sib_copy(i).wait_recv()
            theirs = sib_recv[it, pl.ds(rows_of(i), tile)]
            return mine + theirs

        def to_chips(i, carry):
            x_send[it, pl.ds(pl.multiple_of(i * tile, tile), tile)] = chip_sum(i)
            x_copy(i).start()
            return carry

        def keep(i, carry):
            own[pl.ds(pl.multiple_of((i - n_away) * tile, tile), tile)] = chip_sum(i)
            return carry

        lax.fori_loop(0, n_away, to_sibling, 0)
        lax.fori_loop(0, n_away, to_chips, 0)
        sum_week.spread()
        lax.fori_loop(n_away, n_tiles, to_sibling, 0)
        lax.fori_loop(n_away, n_tiles, keep, 0)
        week_gram = sum_week.result()
        inv = inverse(week_gram, work)

        def a_copy_x(d, q, arriving):
            owner = lax.rem(chip + chips - d, chips) if arriving else chip
            at = pl.ds(pl.multiple_of(core * half + owner * sub + q * tile, tile), tile)
            return pltpu.make_async_remote_copy(
                a_all.at[it, at], a_all.at[it, at],
                ax_sems.at[it, 0, d, q], ax_sems.at[it, 1, d, q],
                device_id={"weeks": lax.rem(chip + d, chips) * 2 + core}, device_id_type=MESH,
            )

        def a_copy_sib(d, q, arriving):
            owner = lax.rem(chip + chips - d, chips)
            part = 1 - core if arriving else core
            at = pl.ds(pl.multiple_of(part * half + owner * sub + q * tile, tile), tile)
            return pltpu.make_async_remote_copy(
                a_all.at[it, at], a_all.at[it, at],
                as_sems.at[it, 0, d, q], as_sems.at[it, 1, d, q],
                device_id={"weeks": chip * 2 + 1 - core}, device_id_type=MESH,
            )

        def update(q, carry):
            at = pl.ds(pl.multiple_of(q * tile, tile), tile)
            total = own[at]
            for d in range(1, chips):
                i = (d - 1) * per_sub + q
                x_copy(i).wait_recv()
                total = total + x_recv[it, pl.ds(pl.multiple_of(i * tile, tile), tile)]
            rows = pl.ds(pl.multiple_of(core * half + chip * sub + q * tile, tile), tile)
            a_all[it, rows] = dot3(total + dot3(a_ref[rows, :], week_gram), inv)
            for d in range(1, chips):
                a_copy_x(d, q, False).start()
            a_copy_sib(0, q, False).start()
            return carry

        lax.fori_loop(0, per_sub, update, 0)
        last = it == ITERS - 1
        if last:
            b_last[...] = b_value
            b_store.start()
        product = jnp.zeros((weeks, rank), jnp.float32)
        gram = jnp.zeros((rank, rank), jnp.float32)
        stored = []
        for d in range(chips):
            owner = lax.rem(chip + chips - d, chips)
            for own_part in (True, False):
                for q in range(per_sub):
                    if not own_part:
                        a_copy_sib(d, q, True).wait_recv()
                    elif d > 0:
                        a_copy_x(d, q, True).wait_recv()
                        a_copy_sib(d, q, False).start()
                part = core if own_part else 1 - core
                at = pl.ds(pl.multiple_of(part * half + owner * sub, sub), sub)
                block = a_all[it, at]
                predicted = dot3(b_value, block, 1, 1)
                if last:
                    k = 2 * d + 1 - int(own_part)
                    imputed[:, at] = base[:, at] + predicted
                    stored += [
                        pltpu.make_async_copy(
                            imputed.at[:, at], hbm_out[0].at[:, at], out_sems.at[2 * k + 1]
                        ),
                        pltpu.make_async_copy(
                            a_all.at[it, at], hbm_out[1].at[at], out_sems.at[2 * k + 2]
                        ),
                    ]
                    stored[-2].start()
                    stored[-1].start()
                else:
                    gram = gram + dot3(block, block, 0, 0)
                    product = product + dot3(cent[:, at] - obs[:, at] * predicted, block)

        def drain_tiles(i, carry):
            sib_copy(i).wait_send()
            return carry

        def drain_away(i, carry):
            x_copy(i).wait_send()
            return carry

        def drain_rows(q, carry):
            for d in range(chips):
                if d > 0:
                    a_copy_x(d, q, False).wait_send()
                a_copy_sib(d, q, False).wait_send()
            return carry

        lax.fori_loop(0, n_tiles, drain_tiles, 0)
        lax.fori_loop(0, n_away, drain_away, 0)
        lax.fori_loop(0, per_sub, drain_rows, 0)
        a_ref = a_all.at[it]

    for j in range(1, nz):
        region_copy(j).wait_send()
    for j in range(1, nw):
        store_copy(j).wait_send()
    for item in sums:
        item.drain()
    for copy in stored:
        copy.wait()
    b_store.wait()


def on_device(nz, nw, outcomes, observed_mask, store_region, store_factor, week_factor):
    weeks, stores = outcomes.shape
    rank = week_factor.shape[1]
    chips = nw // 2
    half = stores // 2
    away = max(half - half // chips, 128)
    tile = min(256, half // chips)
    n_tiles = half // tile
    per_sub = n_tiles // chips
    vmem = lambda *shape: pltpu.VMEM(shape, jnp.float32)
    sems = lambda *shape: pltpu.SemaphoreType.DMA(shape)
    scratch = [
        vmem(weeks, stores), pltpu.VMEM((weeks, stores), jnp.int32),
        pltpu.VMEM((1, stores), jnp.int32),
        vmem(stores, rank), vmem(weeks, rank), vmem(weeks, stores), vmem(weeks, rank),
        sems(5), sems(4 * chips + 1),
        pltpu.VMEM((REGIONS, stores), jnp.bfloat16),
        vmem(weeks, stores), vmem(weeks, stores), vmem(weeks, stores), vmem(weeks, stores),
        vmem(stores, weeks), vmem(stores, weeks),
        vmem(rank, rank),
        vmem(nz, 2 * REGIONS, weeks), vmem(nw, 8, stores // 4), vmem(1, stores),
        sems(2, nz), sems(2, nw),
        vmem(ITERS, half, rank), vmem(ITERS, half, rank),
        vmem(ITERS, away, rank), vmem(ITERS, away, rank),
        vmem(half // chips, rank),
        vmem(ITERS, stores, rank),
        sems(ITERS, 2, n_tiles), sems(ITERS, 2, n_tiles),
        sems(ITERS, 2, chips, per_sub), sems(ITERS, 2, chips, per_sub),
    ]
    for _ in range(ITERS):
        scratch += Sum.scratch(nz, rank) + Sum.scratch(nz, rank) + Sum.scratch(nw, rank)
    shape = lambda *dims: jax.ShapeDtypeStruct(dims, jnp.float32)
    return pl.pallas_call(
        functools.partial(fused, nz, nw, 3 * ITERS),
        out_shape=(shape(weeks, stores), shape(stores, rank), shape(weeks, rank)),
        in_specs=[pl.BlockSpec(memory_space=pltpu.HBM)] * 5,
        out_specs=tuple([pl.BlockSpec(memory_space=pltpu.HBM)] * 3),
        scratch_shapes=scratch,
        compiler_params=pltpu.CompilerParams(
            collective_id=0, has_side_effects=True, vmem_limit_bytes=56 * 1024 * 1024
        ),
    )(outcomes, observed_mask, store_region.reshape(1, stores), store_factor, week_factor)


def solution(mesh):
    placed = (
        P(("groups", "weeks"), "stores"),
        P(("groups", "weeks"), "stores"),
        P("stores"),
        P(("groups", "stores"), None),
        P(("groups", "weeks"), None),
    )
    return jax.shard_map(
        functools.partial(on_device, mesh.shape["stores"], mesh.shape["weeks"]),
        mesh=mesh,
        in_specs=placed,
        out_specs=(
            P(("groups", "weeks"), "stores"),
            P(("groups", "stores"), None),
            P(("groups", "weeks"), None),
        ),
        check_vma=False,
    )
```

```python
import functools

import jax
import jax.numpy as jnp
from jax import lax
from jax.experimental import pallas as pl
from jax.experimental.pallas import tpu as pltpu
from jax.sharding import PartitionSpec as P

REGIONS = 16
ITERS = 2
RIDGE_WEIGHT = 8.0
PANEL = 16
MESH = pl.DeviceIdType.MESH
PRECISE = lax.Precision.HIGHEST


def dot(a, b, ca=1, cb=0):
    return lax.dot_general(
        a, b, (((ca,), (cb,)), ((), ())), precision=PRECISE, preferred_element_type=jnp.float32
    )


def split(x):
    high = x.astype(jnp.bfloat16)
    return high, (x - high.astype(jnp.float32)).astype(jnp.bfloat16)


def dot1(a, b, ca=1, cb=0):
    return lax.dot_general(a, b, (((ca,), (cb,)), ((), ())), preferred_element_type=jnp.float32)


def dot3(a, b, ca=1, cb=0):
    a_high, a_low = split(a)
    b_high, b_low = split(b)
    return (
        dot1(a_high, b_high, ca, cb) + dot1(a_high, b_low, ca, cb) + dot1(a_low, b_high, ca, cb)
    )


def inverse(gram, work):
    rank = gram.shape[0]
    row_at = lax.broadcasted_iota(jnp.int32, (rank, rank), 0)
    lane_at = lax.broadcasted_iota(jnp.int32, (rank, rank), 1)
    work[...] = gram + jnp.where(row_at == lane_at, RIDGE_WEIGHT, 0.0)
    panel_row = lax.broadcasted_iota(jnp.int32, (PANEL, rank), 0)
    panel_lane = lax.broadcasted_iota(jnp.int32, (PANEL, rank), 1)

    def step(_, carry):
        matrix = work[...]
        panel = matrix[:PANEL, :]
        columns = [jnp.broadcast_to(panel[:, j : j + 1], panel.shape) for j in range(PANEL)]
        for k in range(PANEL):
            pivot = 1.0 / columns[k][k : k + 1, :]
            column = columns[k]
            row = jnp.where(panel_lane[:1] == k, pivot, panel[k : k + 1, :] * pivot)
            cleared = jnp.where(panel_lane == k, 0.0, panel)
            panel = jnp.where(panel_row == k, row, cleared - column * row)
            for j in range(k + 1, PANEL):
                scaled = columns[j][k : k + 1, :] * pivot
                columns[j] = jnp.where(panel_row == k, scaled, columns[j] - column * scaled)
        rest = matrix[PANEL:, :]
        kept = jnp.where(lane_at[PANEL:] < PANEL, 0.0, rest)
        rest = kept - dot(rest[:, :PANEL], panel)
        work[...] = pltpu.roll(jnp.concatenate([rest, panel], axis=0), rank - PANEL, 1)
        return carry

    lax.fori_loop(0, rank // PANEL, step, 0)
    return work[...]


class Sum:
    def __init__(self, axis, n, me, refs):
        self.axis, self.n, self.me = axis, n, me
        self.send, self.part, self.full, self.sems = refs
        self.rows = self.send.shape[0] // n
        self.direct = self.rows < 8

    @staticmethod
    def scratch(n, rank):
        rows = rank // n
        part = (n, rank, rank) if rows < 8 else (n, rows, rank)
        return [
            pltpu.VMEM((rank, rank), jnp.float32),
            pltpu.VMEM(part, jnp.float32),
            pltpu.VMEM((rank, rank), jnp.float32),
            pltpu.SemaphoreType.DMA((4, n)),
        ]

    def block(self, ref, owner):
        return ref.at[pl.ds(pl.multiple_of(owner * self.rows, 8), self.rows)]

    def first(self, j):
        peer = lax.rem(self.me + j, self.n)
        source = self.send if self.direct else self.block(self.send, peer)
        return pltpu.make_async_remote_copy(
            source, self.part.at[j], self.sems.at[0, j], self.sems.at[1, j],
            device_id={self.axis: peer}, device_id_type=MESH,
        )

    def second(self, j, arriving):
        owner = lax.rem(self.me + self.n - j, self.n) if arriving else self.me
        peer = lax.rem(self.me + j, self.n)
        block = self.block(self.full, owner)
        return pltpu.make_async_remote_copy(
            block, block, self.sems.at[2, j], self.sems.at[3, j],
            device_id={self.axis: peer}, device_id_type=MESH,
        )

    def start(self, value):
        self.send[...] = value
        for j in range(1, self.n):
            self.first(j).start()

    def spread(self):
        if self.direct:
            return
        total = self.block(self.send, self.me)[...]
        for j in range(1, self.n):
            self.first(j).wait_recv()
            total = total + self.part[j]
        self.block(self.full, self.me)[...] = total
        for j in range(1, self.n):
            self.second(j, False).start()

    def result(self):
        if not self.direct:
            for j in range(1, self.n):
                self.second(j, True).wait_recv()
            return self.full[...]
        for j in range(1, self.n):
            self.first(j).wait_recv()
        self.part[0] = self.send[...]

        def body(t, total):
            return total + self.part[lax.rem(self.n - t + self.me, self.n)]

        return lax.fori_loop(0, self.n, body, jnp.zeros(self.send.shape, jnp.float32))

    def drain(self):
        for j in range(1, self.n):
            self.first(j).wait_send()
            if not self.direct:
                self.second(j, False).wait_send()


def fused(nz, nw, n_sum, *refs):
    hbm_in, (imputed, a_out, b_out) = refs[:5], refs[5:8]
    (outcomes, mask, region, a_first, b_first, in_sems) = refs[8:14]
    refs = refs[14:]
    loads = [
        pltpu.make_async_copy(source, target, in_sems.at[k])
        for k, (source, target) in enumerate(
            zip(hbm_in, (outcomes, mask, region, a_first, b_first))
        )
    ]
    for k in (2, 1, 0, 3, 4):
        loads[k].start()
    (onehot, obs, cent, base, pred, obs_t, cent_t, work, region_buf, store_buf, effect_row,
     region_sems, store_sems) = refs[:13]
    refs = refs[13:]
    (sib_send, sib_recv, x_send, x_recv, own, a_all, sib_sems, x_sems, ax_sems, as_sems) = refs[:10]
    refs = refs[10:]
    z = lax.axis_index("stores")
    w = lax.axis_index("weeks")
    sums = []
    for k in range(4 * ITERS - ITERS):
        over_z = k % 3 < 2
        group = refs[4 * k : 4 * k + 4]
        sums.append(Sum("stores", nz, z, group) if over_z else Sum("weeks", nw, w, group))
    weeks, stores = outcomes.shape
    rank = b_first.shape[1]
    core, chip, chips = lax.rem(w, 2), w // 2, nw // 2
    half = stores // 2
    sub = half // chips
    tile = min(256, sub)
    per_sub = sub // tile
    n_tiles = half // tile
    n_away = n_tiles - per_sub
    wide = stores // 4
    big = stores // 2
    step = stores // 4

    barrier = pltpu.get_barrier_semaphore()
    for j in range(1, nz):
        pl.semaphore_signal(barrier, device_id={"stores": lax.rem(z + j, nz)}, device_id_type=MESH)
    for j in range(1, nw):
        pl.semaphore_signal(barrier, device_id={"weeks": lax.rem(w + j, nw)}, device_id_type=MESH)

    for k in (2, 1, 0):
        loads[k].wait()
    onehot[...] = (
        lax.broadcasted_iota(jnp.int32, (REGIONS, stores), 0) == region[...]
    ).astype(jnp.bfloat16)
    obs[...] = mask[...].astype(jnp.float32)
    high, low = split(obs[...] * outcomes[...])
    total = dot1(onehot[...], high, 1, 1) + dot1(onehot[...], low, 1, 1)
    count = dot1(onehot[...], obs[...].astype(jnp.bfloat16), 1, 1)
    region_buf[0] = jnp.concatenate([total, count], axis=0)
    pl.semaphore_wait(barrier, nz + nw - 2)

    def region_copy(j):
        return pltpu.make_async_remote_copy(
            region_buf.at[0], region_buf.at[j], region_sems.at[0, j], region_sems.at[1, j],
            device_id={"stores": lax.rem(z + j, nz)}, device_id_type=MESH,
        )

    for j in range(1, nz):
        region_copy(j).start()

    def gram_step(t, total):
        block = a_first[pl.ds(pl.multiple_of(t * big, big), big), :]
        return total + dot3(block, block, 0, 0)

    loads[3].wait()
    loads[4].wait()
    zero = jnp.zeros((rank, rank), jnp.float32)
    sums[0].start(lax.fori_loop(0, stores // big, gram_step, zero))

    for j in range(1, nz):
        region_copy(j).wait_recv()

    def add_region(t, total):
        return total + region_buf[lax.rem(z - t + nz, nz)]

    sums_region = lax.fori_loop(
        0, nz, add_region, jnp.zeros(region_buf.shape[1:], jnp.float32)
    )
    effect = (sums_region[:REGIONS] / (sums_region[REGIONS:] + 1.0)).T
    high, low = split(effect)
    base[...] = dot1(high, onehot[...]) + dot1(low, onehot[...])
    store_total = jnp.sum(obs[...] * (outcomes[...] - base[...]), axis=0, keepdims=True)
    store_count = jnp.sum(obs[...], axis=0, keepdims=True)
    for q in range(4):
        store_buf[0, q : q + 1, :] = store_total[:, q * wide : (q + 1) * wide]
        store_buf[0, q + 4 : q + 5, :] = store_count[:, q * wide : (q + 1) * wide]

    def store_copy(j):
        return pltpu.make_async_remote_copy(
            store_buf.at[0], store_buf.at[j], store_sems.at[0, j], store_sems.at[1, j],
            device_id={"weeks": lax.rem(w + j, nw)}, device_id_type=MESH,
        )

    for j in range(1, nw):
        store_copy(j).start()
    sums[0].spread()

    b_value = b_first[...]

    def predict_step(t, carry):
        at = pl.ds(pl.multiple_of(t * step, step), step)
        pred[:, at] = dot3(b_value, a_first[at, :], 1, 1)
        return carry

    lax.fori_loop(0, stores // step, predict_step, 0)

    def turn(source, target):
        def body(t, carry):
            at = pl.ds(pl.multiple_of(t * step, step), step)
            target[at, :] = source[:, at].T
            return carry

        lax.fori_loop(0, stores // step, body, 0)

    turn(obs, obs_t)
    for j in range(1, nw):
        store_copy(j).wait_recv()

    def add_store(t, total):
        return total + store_buf[lax.rem(w - t + nw, nw)]

    sums_store = lax.fori_loop(0, nw, add_store, jnp.zeros(store_buf.shape[1:], jnp.float32))
    effect_s = sums_store[:4] / (sums_store[4:] + 1.0)
    for q in range(4):
        effect_row[:, q * wide : (q + 1) * wide] = effect_s[q : q + 1]
    base[...] = base[...] + effect_row[...]
    cent[...] = obs[...] * (outcomes[...] - base[...])

    def product_step(t, total):
        at = pl.ds(pl.multiple_of(t * big, big), big)
        residual = cent[:, at] - obs[:, at] * pred[:, at]
        return total + dot3(residual, a_first[at, :])

    product = lax.fori_loop(
        0, stores // big, product_step, jnp.zeros((weeks, rank), jnp.float32)
    )
    gram = None
    a_ref = a_first
    for it in range(ITERS):
        sum_gram, sum_product, sum_week = sums[3 * it : 3 * it + 3]
        if it > 0:
            sum_gram.start(gram)
        if weeks < rank:
            product = jnp.concatenate(
                [product, jnp.zeros((rank - weeks, rank), jnp.float32)], axis=0
            )
        sum_product.start(product)
        if it > 0:
            sum_gram.spread()
        gram = sum_gram.result()
        if it == 0:
            turn(cent, cent_t)
        sum_product.spread()
        inv = inverse(gram, work)
        product = sum_product.result()[:weeks]
        b_value = dot(product + dot(b_value, gram), inv)

        sum_week.start(dot(b_value.T, b_value))

        def rows_of(i):
            to = lax.rem(chip + 1 + i // per_sub, chips)
            return pl.multiple_of(to * sub + lax.rem(i, per_sub) * tile, tile)

        def local_product(row):
            at = pl.ds(pl.multiple_of(row, tile), tile)
            predicted = dot3(a_ref[at, :], b_value, 1, 1)
            return dot3(cent_t[at, :] - obs_t[at, :] * predicted, b_value)

        def sib_copy(i):
            at = pl.ds(rows_of(i), tile)
            return pltpu.make_async_remote_copy(
                sib_send.at[it, at], sib_recv.at[it, at],
                sib_sems.at[it, 0, i], sib_sems.at[it, 1, i],
                device_id={"weeks": chip * 2 + 1 - core}, device_id_type=MESH,
            )

        def x_copy(i):
            to = lax.rem(chip + 1 + i // per_sub, chips)
            return pltpu.make_async_remote_copy(
                x_send.at[it, pl.ds(pl.multiple_of(i * tile, tile), tile)],
                x_recv.at[it, pl.ds(pl.multiple_of(i * tile, tile), tile)],
                x_sems.at[it, 0, i], x_sems.at[it, 1, i],
                device_id={"weeks": to * 2 + core}, device_id_type=MESH,
            )

        def to_sibling(i, carry):
            sib_send[it, pl.ds(rows_of(i), tile)] = local_product((1 - core) * half + rows_of(i))
            sib_copy(i).start()
            return carry

        def chip_sum(i):
            mine = local_product(core * half + rows_of(i))
            sib_copy(i).wait_recv()
            theirs = sib_recv[it, pl.ds(rows_of(i), tile)]
            return mine + theirs

        def to_chips(i, carry):
            x_send[it, pl.ds(pl.multiple_of(i * tile, tile), tile)] = chip_sum(i)
            x_copy(i).start()
            return carry

        def keep(i, carry):
            own[pl.ds(pl.multiple_of((i - n_away) * tile, tile), tile)] = chip_sum(i)
            return carry

        lax.fori_loop(0, n_away, to_sibling, 0)
        lax.fori_loop(0, n_away, to_chips, 0)
        lax.fori_loop(n_away, n_tiles, to_sibling, 0)
        sum_week.spread()
        lax.fori_loop(n_away, n_tiles, keep, 0)
        week_gram = sum_week.result()
        inv = inverse(week_gram, work)

        def a_copy_x(d, q, arriving):
            owner = lax.rem(chip + chips - d, chips) if arriving else chip
            at = pl.ds(pl.multiple_of(core * half + owner * sub + q * tile, tile), tile)
            return pltpu.make_async_remote_copy(
                a_all.at[it, at], a_all.at[it, at],
                ax_sems.at[it, 0, d, q], ax_sems.at[it, 1, d, q],
                device_id={"weeks": lax.rem(chip + d, chips) * 2 + core}, device_id_type=MESH,
            )

        def a_copy_sib(d, q, arriving):
            owner = lax.rem(chip + chips - d, chips)
            part = 1 - core if arriving else core
            at = pl.ds(pl.multiple_of(part * half + owner * sub + q * tile, tile), tile)
            return pltpu.make_async_remote_copy(
                a_all.at[it, at], a_all.at[it, at],
                as_sems.at[it, 0, d, q], as_sems.at[it, 1, d, q],
                device_id={"weeks": chip * 2 + 1 - core}, device_id_type=MESH,
            )

        def update(q, carry):
            at = pl.ds(pl.multiple_of(q * tile, tile), tile)
            total = own[at]
            for d in range(1, chips):
                i = (d - 1) * per_sub + q
                x_copy(i).wait_recv()
                total = total + x_recv[it, pl.ds(pl.multiple_of(i * tile, tile), tile)]
            rows = pl.ds(pl.multiple_of(core * half + chip * sub + q * tile, tile), tile)
            a_all[it, rows] = dot3(total + dot3(a_ref[rows, :], week_gram), inv)
            for d in range(1, chips):
                a_copy_x(d, q, False).start()
            a_copy_sib(0, q, False).start()
            return carry

        lax.fori_loop(0, per_sub, update, 0)
        last = it == ITERS - 1
        if last:
            b_out[...] = b_value
        product = jnp.zeros((weeks, rank), jnp.float32)
        gram = jnp.zeros((rank, rank), jnp.float32)
        for d in range(chips):
            owner = lax.rem(chip + chips - d, chips)
            for own_part in (True, False):
                for q in range(per_sub):
                    if not own_part:
                        a_copy_sib(d, q, True).wait_recv()
                    elif d > 0:
                        a_copy_x(d, q, True).wait_recv()
                        a_copy_sib(d, q, False).start()
                part = core if own_part else 1 - core
                at = pl.ds(pl.multiple_of(part * half + owner * sub, sub), sub)
                block = a_all[it, at]
                predicted = dot3(b_value, block, 1, 1)
                if last:
                    imputed[:, at] = base[:, at] + predicted
                    a_out[at, :] = block
                else:
                    gram = gram + dot3(block, block, 0, 0)
                    product = product + dot3(cent[:, at] - obs[:, at] * predicted, block)

        def drain_tiles(i, carry):
            sib_copy(i).wait_send()
            return carry

        def drain_away(i, carry):
            x_copy(i).wait_send()
            return carry

        def drain_rows(q, carry):
            for d in range(chips):
                if d > 0:
                    a_copy_x(d, q, False).wait_send()
                a_copy_sib(d, q, False).wait_send()
            return carry

        lax.fori_loop(0, n_tiles, drain_tiles, 0)
        lax.fori_loop(0, n_away, drain_away, 0)
        lax.fori_loop(0, per_sub, drain_rows, 0)
        a_ref = a_all.at[it]

    for j in range(1, nz):
        region_copy(j).wait_send()
    for j in range(1, nw):
        store_copy(j).wait_send()
    for item in sums:
        item.drain()


def on_device(nz, nw, outcomes, observed_mask, store_region, store_factor, week_factor):
    weeks, stores = outcomes.shape
    rank = week_factor.shape[1]
    chips = nw // 2
    half = stores // 2
    away = max(half - half // chips, 128)
    tile = min(256, half // chips)
    n_tiles = half // tile
    per_sub = n_tiles // chips
    vmem = lambda *shape: pltpu.VMEM(shape, jnp.float32)
    sems = lambda *shape: pltpu.SemaphoreType.DMA(shape)
    scratch = [
        vmem(weeks, stores), pltpu.VMEM((weeks, stores), jnp.int32),
        pltpu.VMEM((1, stores), jnp.int32),
        vmem(stores, rank), vmem(weeks, rank),
        sems(5),
        pltpu.VMEM((REGIONS, stores), jnp.bfloat16),
        vmem(weeks, stores), vmem(weeks, stores), vmem(weeks, stores), vmem(weeks, stores),
        vmem(stores, weeks), vmem(stores, weeks),
        vmem(rank, rank),
        vmem(nz, 2 * REGIONS, weeks), vmem(nw, 8, stores // 4), vmem(1, stores),
        sems(2, nz), sems(2, nw),
        vmem(ITERS, half, rank), vmem(ITERS, half, rank),
        vmem(ITERS, away, rank), vmem(ITERS, away, rank),
        vmem(half // chips, rank),
        vmem(ITERS, stores, rank),
        sems(ITERS, 2, n_tiles), sems(ITERS, 2, n_tiles),
        sems(ITERS, 2, chips, per_sub), sems(ITERS, 2, chips, per_sub),
    ]
    for _ in range(ITERS):
        scratch += Sum.scratch(nz, rank) + Sum.scratch(nz, rank) + Sum.scratch(nw, rank)
    shape = lambda *dims: jax.ShapeDtypeStruct(dims, jnp.float32)
    return pl.pallas_call(
        functools.partial(fused, nz, nw, 3 * ITERS),
        out_shape=(shape(weeks, stores), shape(stores, rank), shape(weeks, rank)),
        in_specs=[pl.BlockSpec(memory_space=pltpu.HBM)] * 5,
        out_specs=tuple([pl.BlockSpec(memory_space=pltpu.VMEM)] * 3),
        scratch_shapes=scratch,
        compiler_params=pltpu.CompilerParams(
            collective_id=0, has_side_effects=True, vmem_limit_bytes=48 * 1024 * 1024
        ),
    )(outcomes, observed_mask, store_region.reshape(1, stores), store_factor, week_factor)


def solution(mesh):
    placed = (
        P(("groups", "weeks"), "stores"),
        P(("groups", "weeks"), "stores"),
        P("stores"),
        P(("groups", "stores"), None),
        P(("groups", "weeks"), None),
    )
    return jax.shard_map(
        functools.partial(on_device, mesh.shape["stores"], mesh.shape["weeks"]),
        mesh=mesh,
        in_specs=placed,
        out_specs=(
            P(("groups", "weeks"), "stores"),
            P(("groups", "stores"), None),
            P(("groups", "weeks"), None),
        ),
        check_vma=False,
    )
```
